128 devices in a mesh: dp: 8 (over z, x_lo), mp: 16 (over y, x_hi, core).
Axes of the slice: x: 4 (x_hi: 2, x_lo: 2; x = x_hi * 2 + x_lo), y: 4, z: 4, core: 2. Of those that a mesh axis runs over, the one named last changes fastest.
Arguments:
- enc_states: bfloat16 [128, 128, 1024], P(('dp', 'mp')), may hold values from -8 to 8
- dec_states: bfloat16 [128, 128, 6144], P('dp', None, 'mp'), may hold values from -8 to 8
- target_rows: int32 [128, 24], P('dp'), may hold values from 0 to 127, as said below
- target_count: int32 [128], P('dp'), may hold values from 3 to 24, as said below
- targets: bfloat16 [128, 24, 6144], P('dp', None, 'mp'), may hold values from -3 to 3
- w_query: bfloat16 [6144, 4096], P('dp', 'mp'), may hold values from -2 to 2
- w_key: bfloat16 [1024, 4096], P('dp', 'mp'), may hold values from -2 to 2
- w_value: bfloat16 [1024, 4096], P('dp', 'mp'), may hold values from -0.1875 to 0.1875
- w_out: bfloat16 [4096, 6144], P('mp', 'dp'), may hold values from -0.09375 to 0.09375
Outputs:
- loss: float32 [], replicated
- row_grads: bfloat16 [128, 24, 6144], P('dp', None, 'mp')
- enc_grads: bfloat16 [128, 128, 1024], P(('dp', 'mp'))
- query_weight_grad: float32 [6144, 4096], P('dp', 'mp')
- key_weight_grad: float32 [1024, 4096], P('dp', 'mp')
- value_weight_grad: float32 [1024, 4096], P('dp', 'mp')
- out_weight_grad: float32 [4096, 6144], P('mp', 'dp')
The draws below stay inside these ranges and needn't reach their ends.
Inputs may be any that keep to these rules, and one draw needn't show every extreme that they name: `target_rows`: each file's row numbers are strictly increasing and come in runs of four consecutive rows that start at multiples of four; only the first target_count entries of a file are targets, the rest are row numbers that carry no target. `target_count`: some file has exactly 24 targets.
All inputs are finite; a program needn't handle non-finite values.
Results may differ from the reference program's by a relative error of at most 0.033.
The reference program's roundings to bfloat16 on the way count: a program that leaves them out, or rounds other values in their place, can miss the bound.
Values may be sent and summed in bfloat16 or wider, within the bound.
No kernel may reach another device: no remote copies, remote signals or barrier semaphores. Data moves between devices by JAX's collectives and lax.ppermute only.
A program may use at most 128 MiB of HBM per device.

```python
import jax
import jax.numpy as jnp
from jax import lax

D = 6144
E = 1024
H = 16
HD = 256
LE = 128
LD = 128
CAP = 24
HW = 4096
FILES = 128
N_DP = 8
N_MP = 16


def span_layout(key):
    count_key, rows_key, pick_key = jax.random.split(key, 3)
    file_ids = jnp.arange(FILES, dtype=jnp.int32)
    span = 4 * (FILES - 1)
    upper = jnp.maximum(1, (CAP * (FILES - 1 + 3 * file_ids) + span - 1) // span)
    lower = jnp.maximum(1, upper // 2)
    counts = jax.random.randint(count_key, (FILES,), lower, upper + 1)
    chosen = FILES - 1 - jax.random.randint(pick_key, (), 0, N_MP)
    counts = jnp.where(file_ids == chosen, CAP, counts).astype(jnp.int32)
    file_keys = jax.random.split(rows_key, FILES)

    def pick_runs(file_key):
        return jax.random.permutation(file_key, LD // 4)[:CAP // 4]
    starts = jnp.sort(jax.vmap(pick_runs)(file_keys), axis=1)
    row_ids = (starts[:, :, None] * 4 + jnp.arange(4)[None, None, :]).reshape(FILES, CAP)
    return (counts, row_ids.astype(jnp.int32))


def draw_target_rows(key, part):
    return span_layout(key)[1]


def draw_target_count(key, part):
    return span_layout(key)[0]


def draw_targets(key, part):
    key = jax.random.fold_in(key, 5)
    file_pos = (jnp.arange(FILES, dtype=jnp.float32) / (FILES - 1))[:, None, None]
    col_pos = (jnp.arange(D, dtype=jnp.float32) / (D - 1))[None, None, :]
    scale = 0.3 * jnp.exp(file_pos * 0.6931472) * jnp.exp(col_pos * 0.6931472)
    sample = jnp.clip(jax.random.normal(key, (FILES, CAP, D), jnp.float32), -2.5, 2.5) * scale
    return sample.astype(jnp.bfloat16)


def draw_w_query(key, part):
    key = jax.random.fold_in(key, 1)
    sample = jax.random.normal(key, (D, HW), jnp.float32) * D ** (-0.5)
    return sample.astype(jnp.bfloat16)


def draw_w_key(key, part):
    key = jax.random.fold_in(key, 2)
    sample = jax.random.normal(key, (E, HW), jnp.float32) * E ** (-0.5)
    return sample.astype(jnp.bfloat16)


def draw_dec_states(key, part):
    key = jax.random.fold_in(key, 3)
    second_key = jax.random.fold_in(key, 1)
    sample = jnp.clip(jax.random.normal(second_key, (FILES, LD, D), jnp.float32), -6.0, 6.0)
    return sample.astype(jnp.bfloat16)


def draw_enc_states(key, part):
    key = jax.random.fold_in(key, 4)
    second_key = jax.random.fold_in(key, 1)
    sample = jnp.clip(jax.random.normal(second_key, (FILES, LE, E), jnp.float32), -6.0, 6.0)
    return sample.astype(jnp.bfloat16)


def shard_levels(stream_key, dims, cuts, low, largest):
    def one(dim, blocks):
        heights = jax.random.uniform(jax.random.fold_in(jax.random.fold_in(stream_key, 6), dim), (blocks,), jnp.float32, low / len(cuts), largest / len(cuts))
        return jnp.repeat(jnp.exp(heights), dims[dim] // blocks).reshape((-1,) + (1,) * (len(dims) - dim - 1))

    factor_of = one(*cuts[0])
    for cut in cuts[1:]:
        factor_of = factor_of * one(*cut)
    return factor_of


def noise(rng, extent, scale, reach, cuts=(), held_as=jnp.bfloat16):
    drawn = scale * jax.random.normal(rng, extent, jnp.float32)
    if cuts:
        drawn = drawn * shard_levels(rng, extent, cuts, -0.22, 0.18)
    return jnp.clip(drawn, -reach, reach).astype(held_as)


def setup_inputs(seed: int = 0) -> dict:
    arg_keys = jax.random.split(jax.random.key(seed), 10)
    enc_states = draw_enc_states(jax.random.fold_in(arg_keys[9], 71), 0)
    dec_states = draw_dec_states(jax.random.fold_in(arg_keys[9], 71), 0)
    target_rows = draw_target_rows(jax.random.fold_in(arg_keys[9], 71), 0)
    target_count = draw_target_count(jax.random.fold_in(arg_keys[9], 71), 0)
    targets = draw_targets(jax.random.fold_in(arg_keys[9], 71), 0)
    w_query = draw_w_query(jax.random.fold_in(arg_keys[9], 71), 0)
    w_key = draw_w_key(jax.random.fold_in(arg_keys[9], 71), 0)
    w_value = noise(arg_keys[7], (E, HW), E ** -0.5, 0.1875, ((0, 8), (1, 16)))
    w_out = noise(arg_keys[8], (HW, D), HW ** -0.5, 0.09375, ((0, 16), (1, 8)))
    return {"enc_states": enc_states, "dec_states": dec_states, "target_rows": target_rows, "target_count": target_count, "targets": targets, "w_query": w_query, "w_key": w_key, "w_value": w_value, "w_out": w_out}


loss_scale = 1024.0


def rounded(values):
    return lax.optimization_barrier(values.astype(jnp.bfloat16)).astype(jnp.float32)


def reference(enc_states, dec_states, target_rows, target_count, targets, w_query, w_key, w_value, w_out):
    inv_root = HD ** -0.5
    head_cols = HW // N_MP
    query_w = w_query.astype(jnp.float32)
    key_w = w_key.astype(jnp.float32)
    value_w = w_value.astype(jnp.float32)
    out_w = w_out.astype(jnp.float32)
    query_groups = query_w.reshape(D, N_MP, head_cols)
    key_groups = key_w.reshape(E, N_MP, head_cols)
    value_groups = value_w.reshape(E, N_MP, head_cols)
    out_groups = out_w.reshape(N_MP, head_cols, D)

    def rank_step(totals, pieces):
        encoder, decoder, row_ids, file_counts, target_vals = pieces
        files_here = encoder.shape[0]
        gathered = jnp.take_along_axis(decoder, row_ids[:, :, None], axis=1).astype(jnp.float32)
        encoded = encoder.astype(jnp.float32)
        queries = rounded(jnp.einsum('fcd,dn->fcn', gathered, query_w))
        key_all = rounded(jnp.einsum('fle,en->fln', encoded, key_w))
        value_all = rounded(jnp.einsum('fle,en->fln', encoded, value_w))
        query_heads = queries.reshape(files_here, CAP, H, HD)
        key_heads = key_all.reshape(files_here, LE, H, HD)
        value_heads = value_all.reshape(files_here, LE, H, HD)
        scores = jnp.einsum('fchd,flhd->fhcl', query_heads, key_heads) * inv_root
        softmaxed = jax.nn.softmax(scores, axis=-1)
        soft_round = rounded(softmaxed)
        attended = rounded(jnp.einsum('fhcl,flhd->fchd', soft_round, value_heads)).reshape(files_here, CAP, HW)
        out_terms = jnp.einsum('fcgn,gnd->fcgd', attended.reshape(files_here, CAP, N_MP, head_cols), out_groups)
        projected = jnp.sum(rounded(out_terms), axis=2)
        target_mask = (jnp.arange(CAP)[None, :] < file_counts[:, None]).astype(jnp.float32)
        residual = target_mask[:, :, None] * (projected - target_vals.astype(jnp.float32))
        squares = jnp.sum(residual * residual)
        residual_round = rounded(residual)
        attended_grad = rounded(jnp.einsum('fcd,nd->fcn', residual_round, out_w))
        grad_heads = attended_grad.reshape(files_here, CAP, H, HD)
        prob_grad = jnp.einsum('fchd,flhd->fhcl', grad_heads, value_heads)
        row_dot = jnp.sum(softmaxed * prob_grad, axis=-1, keepdims=True)
        score_grad = rounded(softmaxed * (prob_grad - row_dot) * inv_root)
        query_grad = rounded(jnp.einsum('fhcl,flhd->fchd', score_grad, key_heads)).reshape(files_here, CAP, HW)
        key_grad = rounded(jnp.einsum('fhcl,fchd->flhd', score_grad, query_heads)).reshape(files_here, LE, HW)
        value_grad = rounded(jnp.einsum('fhcl,fchd->flhd', soft_round, grad_heads)).reshape(files_here, LE, HW)
        row_terms = jnp.einsum('fcgn,dgn->fcgd', query_grad.reshape(files_here, CAP, N_MP, head_cols), query_groups)
        row_part = jnp.sum(rounded(row_terms), axis=2)
        enc_terms = jnp.einsum('flgn,egn->flge', key_grad.reshape(files_here, LE, N_MP, head_cols), key_groups)
        enc_terms = enc_terms + jnp.einsum('flgn,egn->flge', value_grad.reshape(files_here, LE, N_MP, head_cols), value_groups)
        enc_part = jnp.sum(rounded(enc_terms), axis=2)
        query_total = totals[0] + rounded(jnp.einsum('fcd,fcn->dn', gathered, query_grad))
        key_total = totals[1] + rounded(jnp.einsum('fle,fln->en', encoded, key_grad))
        value_total = totals[2] + rounded(jnp.einsum('fle,fln->en', encoded, value_grad))
        out_total = totals[3] + rounded(jnp.einsum('fcn,fcd->nd', attended, residual_round))
        return (query_total, key_total, value_total, out_total), (row_part, enc_part, squares)

    start_totals = (jnp.zeros((D, HW), jnp.float32), jnp.zeros((E, HW), jnp.float32),
                    jnp.zeros((E, HW), jnp.float32), jnp.zeros((HW, D), jnp.float32))
    sliced = (enc_states.reshape(N_DP, N_MP, LE, E), dec_states.reshape(N_DP, N_MP, LD, D),
              target_rows.reshape(N_DP, N_MP, CAP), target_count.reshape(N_DP, N_MP),
              targets.reshape(N_DP, N_MP, CAP, D))
    totals, stacked = lax.scan(rank_step, start_totals, sliced)
    row_parts, enc_parts, square_parts = stacked
    target_total = jnp.sum(target_count).astype(jnp.float32)
    grad_factor = loss_scale / target_total
    loss = jnp.sum(square_parts) / (2.0 * D * target_total)
    row_grads = (row_parts.reshape(FILES, CAP, D) * grad_factor).astype(jnp.bfloat16)
    enc_grads = (enc_parts.reshape(FILES, LE, E) * grad_factor).astype(jnp.bfloat16)
    return (loss, row_grads, enc_grads, totals[0] * grad_factor, totals[1] * grad_factor,
            totals[2] * grad_factor, totals[3] * grad_factor)
```

```python
import functools

import jax
import jax.numpy as jnp
from jax import lax
from jax.experimental import pallas as pl
from jax.experimental.pallas import tpu as pltpu
from jax.sharding import PartitionSpec as P

D = 6144
HD = 256
N_Z, N_Y = 4, 4

loss_scale = 1024.0
bf16, f32 = jnp.bfloat16, jnp.float32


def mp_table(step):
    pairs = []
    for i in range(4 * N_Y):
        y, h, c = step(i // 4, i // 2 % 2, i % 2)
        pairs.append((i, y % N_Y * 4 + h % 2 * 2 + c % 2))
    return pairs


def dp_table(step):
    pairs = []
    for i in range(2 * N_Z):
        z, l = step(i // 2, i % 2)
        pairs.append((i, z % N_Z * 2 + l % 2))
    return pairs


CORE = ("mp", mp_table(lambda y, h, c: (y, h, c + 1)))
XH = ("mp", mp_table(lambda y, h, c: (y, h + 1, c)))
Y_UP = ("mp", mp_table(lambda y, h, c: (y + 1, h, c)))
Y_DOWN = ("mp", mp_table(lambda y, h, c: (y - 1, h, c)))
XL = ("dp", dp_table(lambda z, l: (z, l + 1)))
Z_UP = ("dp", dp_table(lambda z, l: (z + 1, l)))
Z_DOWN = ("dp", dp_table(lambda z, l: (z - 1, l)))
TURN = (("dp", "mp"), [(g * 16 + m, m // 2 * 16 + 2 * g + m % 2) for g in range(8) for m in range(16)])


def send(x, route):
    return lax.ppermute(x, *route)


def add(*terms):
    total = terms[0].astype(f32)
    for term in terms[1:]:
        total = total + term.astype(f32)
    return total.astype(bf16)


def ring_gather(block, up, down):
    below = send(block, up)
    above = send(block, down)
    far_first = send(below[0], up)
    far_second = send(above[1], down)
    return jnp.stack([block, above, jnp.stack([far_first, far_second]), below])


def pair_gather(own, route):
    return jnp.stack([own, send(own, route)])


def gather_mp(own):
    ring = ring_gather(pair_gather(own, XH), Y_UP, Y_DOWN)
    return pair_gather(ring, CORE)


def gather_dp(own):
    return ring_gather(pair_gather(own, XL), Z_UP, Z_DOWN)


def ring_scatter(terms, up, down):
    up_first = send(terms[2, 0], up)
    down_second = send(terms[2, 1], down)
    from_below = send(jnp.stack([add(terms[1, 0], up_first), terms[1, 1]]), up)
    from_above = send(jnp.stack([terms[3, 0], add(terms[3, 1], down_second)]), down)
    return add(terms[0], from_below, from_above)


def scatter_mp(other, mine):
    pair = ring_scatter(add(mine, send(other, CORE)), Y_UP, Y_DOWN)
    return pair[0].astype(f32) + send(pair[1], XH).astype(f32)


def scatter_dp(terms):
    pair = ring_scatter(terms, Z_UP, Z_DOWN)
    return pair[0].astype(f32) + send(pair[1], XL).astype(f32)


PARAMS = pltpu.CompilerParams(vmem_limit_bytes=48 * 2**20)


def sum_kernel(order, left, right, out, total):
    step = pl.program_id(0)

    @pl.when(step == 0)
    def _():
        total[...] = jnp.zeros_like(total)

    for k in range(2):
        total[...] += jnp.dot(left[k, 0], right[0, k], preferred_element_type=f32)

    @pl.when(step == pl.num_programs(0) - 1)
    def _():
        out[...] = total[...].astype(out.dtype)


def sum_of_products(order, left, right, dtype):
    _, n, rows, depth = left.shape
    columns = right.shape[-1]
    return pl.pallas_call(
        sum_kernel,
        grid_spec=pltpu.PrefetchScalarGridSpec(
            num_scalar_prefetch=1,
            grid=(n,),
            in_specs=[
                pl.BlockSpec((2, 1, rows, depth), lambda p, order: (0, p, 0, 0)),
                pl.BlockSpec((1, 2, depth, columns), lambda p, order: (order[p], 0, 0, 0)),
            ],
            out_specs=pl.BlockSpec((rows, columns), lambda p, order: (0, 0)),
            scratch_shapes=[pltpu.VMEM((rows, columns), f32)],
        ),
        out_shape=jax.ShapeDtypeStruct((rows, columns), dtype),
        compiler_params=PARAMS,
        cost_estimate=pl.CostEstimate(
            flops=4 * n * rows * depth * columns,
            bytes_accessed=4 * n * depth * (rows + columns) + 4 * rows * columns,
            transcendentals=0,
        ),
    )(order, left, right)


def spread_kernel(order, left, right, out):
    out[0] = lax.dot_general(
        left[...], right[0, 0], (((1,), (1,)), ((), ())), preferred_element_type=f32
    ).astype(out.dtype)


def spread_products(order, left, right, k):
    rows, depth = left.shape
    n, _, columns, _ = right.shape
    return pl.pallas_call(
        spread_kernel,
        grid_spec=pltpu.PrefetchScalarGridSpec(
            num_scalar_prefetch=1,
            grid=(n,),
            in_specs=[
                pl.BlockSpec((rows, depth), lambda p, order: (0, 0)),
                pl.BlockSpec((1, 1, columns, depth), lambda p, order: (order[p], k, 0, 0)),
            ],
            out_specs=pl.BlockSpec((1, rows, columns), lambda p, order: (p, 0, 0)),
        ),
        out_shape=jax.ShapeDtypeStruct((n, rows, columns), bf16),
        compiler_params=PARAMS,
        cost_estimate=pl.CostEstimate(
            flops=2 * n * rows * depth * columns,
            bytes_accessed=2 * n * (rows + depth) * columns,
            transcendentals=0,
        ),
    )(order, left, right)


def weight_kernel(place, left, right, out):
    for k in range(2):
        out[0, k] = lax.dot_general(
            left[k, 0], right[...], (((0,), (0,)), ((), ())), preferred_element_type=f32
        ).astype(out.dtype)


def weight_products(place, left, right):
    _, n, rows, depth = left.shape
    columns = right.shape[-1]
    return pl.pallas_call(
        weight_kernel,
        grid_spec=pltpu.PrefetchScalarGridSpec(
            num_scalar_prefetch=1,
            grid=(n,),
            in_specs=[
                pl.BlockSpec((2, 1, rows, depth), lambda q, place: (0, place[q], 0, 0)),
                pl.BlockSpec((rows, columns), lambda q, place: (0, 0)),
            ],
            out_specs=pl.BlockSpec((1, 2, depth, columns), lambda q, place: (q, 0, 0, 0)),
        ),
        out_shape=jax.ShapeDtypeStruct((n, 2, depth, columns), bf16),
        compiler_params=PARAMS,
        cost_estimate=pl.CostEstimate(
            flops=4 * n * rows * depth * columns,
            bytes_accessed=4 * n * depth * (rows + columns),
            transcendentals=0,
        ),
    )(place, left, right)


def total_over(x, routes):
    for route in routes:
        x = x + send(x, route)
    return x


def shards(
    enc_states, dec_states, target_rows, target_count, targets, w_query, w_key, w_value, w_out
):
    inv_root = HD ** (-0.5)
    files = dec_states.shape[0]
    tokens = enc_states.shape[1]
    slots = target_rows.shape[1]
    rows = files * slots
    width = dec_states.shape[2]
    g = lax.axis_index("dp")
    m = lax.axis_index("mp")
    z, l = g // 2, g % 2
    y, h, c = m // 4, m // 2 % 2, m % 2
    eight = jnp.arange(8)
    mp_index = (y + eight // 2) % 4 * 2 + (h + eight) % 2
    dp_index = (z + eight // 2) % 4 * 2 + (l + eight) % 2
    dp_place = (eight // 2 - z) % 4 * 2 + (eight + l) % 2
    mp_place = (eight // 2 - y) % 4 * 2 + (eight + h) % 2
    order = dp_place[mp_index].astype(jnp.int32)
    place = mp_place[dp_index].astype(jnp.int32)
    file_of = jnp.concatenate([mp_index * 2 + c, mp_index * 2 + 1 - c])
    pick = (file_of[:, None] == jnp.arange(files)[None, :]).astype(bf16)

    def core_order(x):
        return jnp.where(c == 0, x, x[::-1])

    with jax.named_scope("gather_kv_weights"):
        pair_own = jnp.concatenate([w_key, w_value], axis=1)
        pair_ring = gather_dp(pair_own).reshape(8, *pair_own.shape)
        pair_full = pair_ring[dp_place].reshape(-1, pair_own.shape[1])
    with jax.named_scope("gather_enc"):
        encoder = gather_mp(enc_states[0]).reshape(16 * tokens, -1)
    with jax.named_scope("gather_rows"):
        own_rows = jnp.take_along_axis(dec_states, target_rows[:, :, None], axis=1)
        rows_all = gather_mp(own_rows.reshape(rows, width)).reshape(2, 8, rows, width)
    with jax.named_scope("gather_w_query"):
        query_w = gather_dp(core_order(w_query.reshape(2, width, HD))).reshape(8, 2, width, HD)
    with jax.named_scope("gather_w_out"):
        halves = core_order(jnp.stack([w_out[:, :width], w_out[:, width:]]))
        got = send(halves[1], CORE)
        column_own = send(jnp.stack([halves[0], got]), TURN)
        out_w = gather_dp(column_own).reshape(8, 2, HD, width)

    with jax.named_scope("attention"):
        key_value = jnp.dot(encoder, pair_full, preferred_element_type=f32).astype(bf16)
        keys = key_value[:, :HD].reshape(files, tokens, HD)
        values = key_value[:, HD:].reshape(files, tokens, HD)
        queries = sum_of_products(order, rows_all, query_w, bf16)

        def to_ring(x):
            return jnp.einsum("ef,fcn->ecn", pick, x.reshape(files, slots, -1), preferred_element_type=f32).astype(bf16)

        def from_ring(x):
            return jnp.einsum("ef,ecn->fcn", pick, x, preferred_element_type=f32).astype(bf16).reshape(rows, -1)

        query_heads = to_ring(queries)
        scores = jnp.einsum("fcd,fld->fcl", query_heads, keys, preferred_element_type=f32) * inv_root
        softmaxed = jax.nn.softmax(scores, axis=-1)
        soft_round = softmaxed.astype(bf16)
        attended = jnp.einsum("fcl,fld->fcd", soft_round, values, preferred_element_type=f32).astype(bf16)
    with jax.named_scope("gather_attended"):
        attended_all = gather_mp(from_ring(attended)).reshape(2, 8, rows, HD)
    with jax.named_scope("residual"):
        projected = sum_of_products(order, attended_all, out_w, f32)
        mask = (jnp.arange(slots)[None, :] < target_count[:, None]).astype(f32)
        residual = mask[:, :, None] * (projected.reshape(files, slots, width) - targets.astype(f32))
        squares = jnp.sum(residual * residual)
        residual_round = residual.astype(bf16).reshape(rows, width)
    with jax.named_scope("scatter_attended_grad"):
        grad_other = spread_products(order, residual_round, out_w, 1)
        grad_mine = spread_products(order, residual_round, out_w, 0)
        attended_grad = scatter_mp(
            grad_other.reshape(4, 2, rows, HD), grad_mine.reshape(4, 2, rows, HD)
        ).astype(bf16)
    with jax.named_scope("totals"):
        counted = jnp.sum(target_count).astype(f32)
        lanes = jnp.arange(128)[None, :]
        both = jnp.where(lanes == 0, counted, jnp.where(lanes == 1, squares, 0.0)) * jnp.ones((8, 1), f32)
        both = total_over(both, [XL, Z_UP])
        both = both + send(send(both, Z_UP), Z_UP)
        target_total = both[0, 0]
        both = total_over(both, [CORE, XH, Y_UP])
        both = both + send(send(both, Y_UP), Y_UP)
        total_squares = both[0, 1]
        grad_factor = loss_scale / target_total
        loss = total_squares / (2.0 * D * target_total)
    with jax.named_scope("scatter_out_weight"):
        out_terms = weight_products(place, attended_all, residual_round)
        out_sum = scatter_dp(out_terms.reshape(4, 2, 2, HD, width))
        turned = send(out_sum.astype(bf16), TURN)
        back = send(turned[1], CORE)
        out_halves = core_order(jnp.stack([turned[0], back]))
        out_weight_grad = jnp.concatenate([out_halves[0], out_halves[1]], axis=1).astype(f32) * grad_factor
    with jax.named_scope("attention_grad"):
        grad_heads = to_ring(attended_grad)
        prob_grad = jnp.einsum("fcd,fld->fcl", grad_heads, values, preferred_element_type=f32)
        row_dot = jnp.sum(softmaxed * prob_grad, axis=-1, keepdims=True)
        score_grad = (softmaxed * (prob_grad - row_dot) * inv_root).astype(bf16)
        query_grad = from_ring(
            jnp.einsum("fcl,fld->fcd", score_grad, keys, preferred_element_type=f32).astype(bf16)
        )
        key_grad = jnp.einsum("fcl,fcd->fld", score_grad, query_heads, preferred_element_type=f32).astype(bf16)
        value_grad = jnp.einsum("fcl,fcd->fld", soft_round, grad_heads, preferred_element_type=f32).astype(bf16)
        pair_grad = jnp.concatenate([key_grad, value_grad], axis=2).reshape(files * tokens, 2 * HD)
    with jax.named_scope("scatter_query_weight"):
        query_terms = weight_products(place, rows_all, query_grad)
        query_sum = scatter_dp(query_terms.reshape(4, 2, 2, width, HD))
        query_weight_grad = (core_order(query_sum) * grad_factor).reshape(2 * width, HD)
    with jax.named_scope("scatter_kv_weights"):
        pair_terms = lax.dot_general(
            encoder, pair_grad, (((0,), (0,)), ((), ())), preferred_element_type=f32
        ).astype(bf16)
        pair_terms = pair_terms.reshape(8, -1, 2 * HD)[dp_index]
        pair_sum = scatter_dp(pair_terms.reshape(4, 2, -1, 2 * HD)) * grad_factor
    with jax.named_scope("scatter_enc"):
        enc_terms = lax.dot_general(
            pair_grad, pair_full, (((1,), (1,)), ((), ())), preferred_element_type=f32
        ).astype(bf16)
        enc_terms = enc_terms.reshape(2, 4, 2, tokens, -1)
        enc_grads = (scatter_mp(enc_terms[1], enc_terms[0]) * grad_factor).astype(bf16)[None]
    with jax.named_scope("scatter_rows"):
        row_other = spread_products(order, query_grad, query_w, 1).reshape(4, 2, rows, width)
        row_mine = spread_products(order, query_grad, query_w, 0).reshape(4, 2, rows, width)
        row_sum = scatter_mp(row_other, row_mine)
        row_grads = (row_sum * grad_factor).astype(bf16).reshape(files, slots, width)
    return (
        loss,
        row_grads,
        enc_grads,
        query_weight_grad,
        pair_sum[:, :HD],
        pair_sum[:, HD:],
        out_weight_grad,
    )


def solution(mesh):
    return jax.shard_map(
        shards,
        mesh=mesh,
        in_specs=(
            P(("dp", "mp"), None, None),
            P("dp", None, "mp"),
            P("dp", None),
            P("dp"),
            P("dp", None, "mp"),
            P("dp", "mp"),
            P("dp", "mp"),
            P("dp", "mp"),
            P("mp", "dp"),
        ),
        out_specs=(
            P(),
            P("dp", None, "mp"),
            P(("dp", "mp"), None, None),
            P("dp", "mp"),
            P("dp", "mp"),
            P("dp", "mp"),
            P("mp", "dp"),
        ),
        check_vma=False,
    )
```
